32 devices in a mesh: stream: 8 (over y, x, core), cross: 4 (over z).
Axes of the slice: x: 2, y: 2, z: 4, core: 2. Of those that a mesh axis runs over, the one named last changes fastest.
Arguments:
- initial_state: float32 [5, 64, 32768], P(None, 'stream', 'cross'), may hold values from -6 to 6
- forcing: float32 [5, 64, 32768], P(None, 'stream', 'cross'), may hold values from -0.3 to 0.3
- block_inverse: float32 [5, 5, 64, 32768], P(None, None, 'stream', 'cross'), may hold values from -1 to 1, as said below
- lower_decay: float32 [5, 64, 32768], P(None, 'stream', 'cross'), may hold values from 0 to 1
- upper_decay: float32 [5, 64, 32768], P(None, 'stream', 'cross'), may hold values from 0 to 1
- cross_coupling: float32 [64, 32768], P('stream', 'cross'), may hold values from 0.002 to 0.02
- iblank: int32 [64, 32768], P('stream', 'cross'), may hold values 0 or 1
- donor_receiver: int32 [1024, 1], P(('stream', 'cross')), may hold values from 0 to 31; in each aligned block of 32 rows (0 to 31, 32 to 63, ...) at most 2 rows name the same one
- donor_block: int32 [1024], P(('stream', 'cross')), may hold values from 0 to 511
- stencil_offset: int32 [1024], P(('stream', 'cross')), may hold values from 1 to 127
- stencil_weight: float32 [1024, 128], P(('stream', 'cross')), may hold values from 0.005 to 0.02
- fringe_target: int32 [2048], P(('stream', 'cross')), may hold values from 0 to 511
Outputs:
- final_state: float32 [5, 64, 32768], P(None, 'stream', 'cross')
- last_update: float32 [5, 64, 32768], P(None, 'stream', 'cross')
The draws below stay inside these ranges and needn't reach their ends.
Inputs may be any that keep to these rules, and one draw needn't show every extreme that they name: `donor_receiver`: within the rows of one device no receiving device is named more than 2 times. `block_inverse`: each 5 x 5 block is orthogonal and symmetric.
All inputs are finite; a program needn't handle non-finite values. No bound on the sum of `iblank` on one device may be relied on, other than what follows from the above.
Results may differ from the reference program's by a relative error of at most 0.00018.
Values sent between devices are 32-bit elements; how exact they have to be, the bound alone decides.
A program may use at most 128 MiB of HBM per device.

```python
import math
import jax
import jax.numpy as jnp
import numpy as np
from jax import lax

CX = 8
CC = 8192
ITERS = 2
CAP = 2
SEND = 32
NX = 64
NC = 32768
NB = 512
N_STREAM = 8
N_CROSS = 4


def draw_block_inverse(key, part):
    vector = jax.random.normal(key, (5, NX, NC), jnp.float32)
    length = jnp.sum(vector * vector, axis=0) + 1e-06
    identity = jnp.eye(5, dtype=jnp.float32)[:, :, None, None]
    return identity - 2.0 * vector[:, None] * vector[None, :] / length[None, None]


def decay_field(key):
    keys = jax.random.split(key, 3)
    low = 0.5 / NX
    high = 1.0 / 30.0
    spread = jax.random.uniform(keys[0], (5, 1, NC), jnp.float32, jnp.log(low), jnp.log(high))
    factor = jnp.broadcast_to(jnp.exp(-jnp.exp(spread)), (5, NX, NC))
    spots = jax.random.randint(keys[1], (3, 5, 1, NC), 0, NX)
    planes = lax.broadcasted_iota(jnp.int32, (5, NX, NC), 1)
    struck = jnp.any(planes[None] == spots, axis=0)
    drop = jax.random.uniform(keys[2], (5, NX, NC), jnp.float32, 0.5, 0.8)
    return jnp.where(struck, factor * drop, factor)


def draw_lower_decay(key, part):
    return decay_field(jax.random.fold_in(key, 11))


def draw_upper_decay(key, part):
    return decay_field(jax.random.fold_in(key, 23))


def plant(entries, rng, least, top_value):
    place = [jax.random.randint(jax.random.fold_in(rng, axis), (), 0, length) for axis, length in enumerate(entries.shape)]
    widest = entries.shape.index(max(entries.shape))
    neighbour = place[:widest] + [(place[widest] + 1) % entries.shape[widest]] + place[widest + 1:]
    return entries.at[tuple(place)].set(least).at[tuple(neighbour)].set(top_value)


def block_levels(rng, extent, shards, smallest, top_value):
    level = 1.0
    for axis_at, shards_of in shards:
        steps = jax.random.uniform(jax.random.fold_in(jax.random.fold_in(rng, 6), axis_at), (shards_of,), jnp.float32, smallest / len(shards), top_value / len(shards))
        level = level * jnp.repeat(jnp.exp(steps), extent[axis_at] // shards_of).reshape((-1,) + (1,) * (len(extent) - 1 - axis_at))
    return level


def shared_out(own_key, own, number, rows, number_of, top, limit, lean):
    order = jax.random.permutation(own_key, number_of)
    packed, common = shares(number_of, rows * top, limit, lean, True), shares(number_of, rows * top, limit, lean, False)
    places = jnp.arange(number_of)

    def named(tallies, turn):
        used = int((tallies > 0).sum())
        fixed = max(1, used // 4)
        passed = fixed + (places - fixed + turn * (used - fixed)) % max(1, number_of - fixed)
        return jnp.zeros((number_of,), jnp.int32).at[order[jnp.where(places < fixed, places, passed)]].set(jnp.asarray(tallies, jnp.int32))

    tallies = jnp.where(number % 4 == 0, named(packed, number // 4), named(common, number - number // 4 - 1))
    mixed = jax.random.permutation(jax.random.fold_in(own, 3), number_of)
    source_of, taker = mixed[0:number_of // 2 * 2:2], mixed[1:number_of // 2 * 2:2]
    slack = jnp.minimum(tallies[source_of] - 1, limit - tallies[taker]) // 2
    slack = jnp.where((source_of == order[0]) | (taker == order[0]) | (tallies[taker] == 0), 0, jnp.maximum(slack, 0))
    passed = jax.random.randint(jax.random.fold_in(own, 4), (number_of // 2,), 0, 1 << 20) % (slack + 1)
    tallies = tallies.at[source_of].add(-passed).at[taker].add(passed)
    labels = jnp.searchsorted(jnp.cumsum(tallies), jnp.arange(rows * top), side="right").astype(jnp.int32)
    listing = labels.reshape(top, rows).T
    listing = listing[jax.random.permutation(jax.random.fold_in(own, 1), rows)]
    turn = jax.random.randint(jax.random.fold_in(own, 2), (rows, 1), 0, top)
    return jnp.take_along_axis(listing, (jnp.arange(top)[None, :] + turn) % top, axis=1)


def shares(amount, total, most, skew, full):
    weights = [(1 << 20) // math.isqrt(rank ** skew) + 1 for rank in range(1, amount + 1)]
    largest = most if full else min(most, max(-(-total // amount), total * weights[0] // sum(weights)))
    least = 1 if total - largest >= amount - 1 else 0
    counts, surplus = [largest] + [least] * (amount - 1), total - largest - least * (amount - 1)
    while surplus > 0:
        candidates = [i for i in range(1, amount) if counts[i] < largest] or [i for i in range(1, amount) if counts[i] < most]
        pool, remaining = sum([weights[i] for i in candidates]), surplus
        for i in candidates:
            extra = min(most - counts[i], max(1, remaining * weights[i] // pool), surplus)
            counts[i] = counts[i] + extra
            surplus = surplus - extra
    return np.array(counts)


def scatter_about(rng, dims, width, bound, pieces=(), held_as=jnp.bfloat16):
    result = width * jax.random.normal(rng, dims, jnp.float32)
    if pieces:
        result = result * block_levels(rng, dims, pieces, -0.22, 0.18)
    return jnp.clip(result, -bound, bound).astype(held_as)


def setup_inputs(seed: int = 0) -> dict:
    key_of = jax.random.split(jax.random.key(seed), 13)
    initial_state = scatter_about(key_of[0], (5, NX, NC), 1.0, 6.0, ((1, 8), (2, 4)), jnp.float32)
    forcing = scatter_about(key_of[1], (5, NX, NC), 0.05, 0.3, ((1, 8), (2, 4)), jnp.float32)
    block_inverse = draw_block_inverse(jax.random.fold_in(key_of[12], 71), 0)
    lower_decay = draw_lower_decay(jax.random.fold_in(key_of[12], 71), 0)
    upper_decay = draw_upper_decay(jax.random.fold_in(key_of[12], 71), 0)
    cross_coupling = jnp.clip(jnp.exp(math.log(0.02) - 2.30258502 * jax.random.uniform(key_of[5], (NX, NC), jnp.float32) ** block_levels(key_of[5], (NX, NC), ((0, 8), (1, 4)), -0.2, 0.2)), 0.002, 0.02)
    iblank = plant((jax.random.randint(key_of[6], (NX, NC), 0, 4) < 3).astype(jnp.int32), jax.random.fold_in(key_of[6], 1), 0, 1)
    donor_receiver_keys = jax.random.split(jax.random.fold_in(key_of[7], 1), (N_STREAM * N_CROSS * SEND) // SEND)
    donor_receiver_turns = jax.random.permutation(jax.random.fold_in(key_of[7], 3), (N_STREAM * N_CROSS * SEND) // SEND)
    donor_receiver = jax.vmap(lambda own, number: shared_out(jax.random.fold_in(key_of[7], 2), own, number, SEND, N_STREAM * N_CROSS, 1, CAP, 2))(donor_receiver_keys, donor_receiver_turns).reshape((N_STREAM * N_CROSS * SEND, 1))
    donor_block = plant(jax.random.randint(key_of[8], (N_STREAM * N_CROSS * SEND,), 0, NB), jax.random.fold_in(key_of[8], 1), 0, NB - 1).astype(jnp.int32)
    stencil_offset = plant(jax.random.randint(key_of[9], (N_STREAM * N_CROSS * SEND,), 1, 128), jax.random.fold_in(key_of[9], 1), 1, 127).astype(jnp.int32)
    stencil_weight = jnp.clip(0.005 + 0.015 * jax.random.uniform(key_of[10], (N_STREAM * N_CROSS * SEND, 128), jnp.float32) ** block_levels(key_of[10], (N_STREAM * N_CROSS * SEND, 128), ((0, 32),), -0.2, 0.2), 0.005, 0.02)
    fringe_target = plant(jax.random.randint(key_of[11], (N_STREAM * N_CROSS * N_STREAM * N_CROSS * CAP,), 0, NB), jax.random.fold_in(key_of[11], 1), 0, NB - 1).astype(jnp.int32)
    return dict(initial_state=initial_state, forcing=forcing, block_inverse=block_inverse, lower_decay=lower_decay, upper_decay=upper_decay, cross_coupling=cross_coupling, iblank=iblank, donor_receiver=donor_receiver, donor_block=donor_block, stencil_offset=stencil_offset, stencil_weight=stencil_weight, fringe_target=fringe_target)


def apply_block(block_inv, vector):
    return jnp.sum(block_inv * vector[None], axis=1)


def fringe_source(state, donor_receiver, donor_block, stencil_offset, stencil_weight, fringe_target):
    devices = N_STREAM * N_CROSS
    block_count = CX * CC // 128
    local = state.reshape(5, N_STREAM, CX, N_CROSS, CC // 128, 128).transpose(1, 3, 0, 2, 4, 5)
    local = local.reshape(devices, 5, block_count, 128)
    rows = devices * SEND
    owner = (jnp.arange(rows, dtype=jnp.int32) // SEND).astype(jnp.int32)
    selected_values = local[owner, :, donor_block]
    lanes = jnp.arange(128, dtype=jnp.int32)[None, :]
    positions = (lanes + stencil_offset[:, None]) % 128
    displaced_values = jnp.take_along_axis(selected_values, jnp.broadcast_to(positions[:, None, :], selected_values.shape), axis=2)
    values = stencil_weight[:, None, :] * (selected_values + displaced_values)
    receiver = donor_receiver[:, 0]
    grouped = receiver.reshape(devices, SEND)
    order = jnp.arange(SEND, dtype=jnp.int32)
    same = grouped[:, :, None] == grouped[:, None, :]
    earlier = order[None, :] < order[:, None]
    slot_rank = jnp.sum((same & earlier[None]).astype(jnp.int32), axis=2).reshape(rows)
    target = fringe_target[receiver * (devices * CAP) + owner * CAP + slot_rank]
    global_block = receiver * block_count + target
    summed = jax.ops.segment_sum(values, global_block, num_segments=devices * block_count)
    summed = summed.reshape(N_STREAM, N_CROSS, CX, CC // 128, 5, 128).transpose(4, 0, 2, 1, 3, 5)
    return summed.reshape(5, NX, NC)


def reference(initial_state, forcing, block_inverse, lower_decay, upper_decay, cross_coupling, iblank, donor_receiver, donor_block, stencil_offset, stencil_weight, fringe_target):
    hole = (1 - iblank).astype(jnp.float32)
    plane_inverses = block_inverse.transpose(2, 0, 1, 3)
    lower_planes = lower_decay.transpose(1, 0, 2)
    upper_planes = upper_decay.transpose(1, 0, 2)

    def forward_step(carry, plane):
        driving_plane, inverse, factor = plane
        near = apply_block(inverse, driving_plane + factor * carry)
        return near, near

    def backward_step(carry, plane):
        near_plane, inverse, factor = plane
        update = near_plane + apply_block(inverse, factor * carry)
        return update, update

    state = initial_state
    update = jnp.zeros_like(initial_state)
    for relaxation_round in range(ITERS):
        laplace = 2.0 * state - jnp.roll(state, 1, axis=2) - jnp.roll(state, -1, axis=2)
        fringe = fringe_source(state, donor_receiver, donor_block, stencil_offset, stencil_weight, fringe_target)
        driving_term = forcing - cross_coupling[None] * laplace + hole[None] * fringe
        start = jnp.zeros((5, NC), jnp.float32)
        _, near = lax.scan(forward_step, start, (driving_term.transpose(1, 0, 2), plane_inverses, lower_planes))
        _, update = lax.scan(backward_step, start, (near, plane_inverses, upper_planes), reverse=True)
        update = update.transpose(1, 0, 2)
        state = state + update
    return state, update
```

```python
import functools

import jax
import jax.numpy as jnp
from jax import lax
from jax.experimental import pallas as pl
from jax.experimental.pallas import tpu as pltpu
from jax.sharding import PartitionSpec as P

ITERS = 2
CAP = 2
NV = 5
SLOT_ROWS = 16
STEP = 16
CHUNKS = 4
MESH = pl.DeviceIdType.MESH
PAIRS = [(a, b) for a in range(NV) for b in range(a, NV)]


def pair(a, b):
    return PAIRS.index((min(a, b), max(a, b)))


def split3(x):
    high = x.astype(jnp.bfloat16)
    rest = x - high.astype(jnp.float32)
    mid = rest.astype(jnp.bfloat16)
    low = (rest - mid.astype(jnp.float32)).astype(jnp.bfloat16)
    return jnp.concatenate([high, mid, low], axis=0)


def iota(shape, dim):
    return lax.broadcasted_iota(jnp.int32, shape, dim)


def kernel(
    ns, nc, planes, tiles,
    state_h, forcing_h, inverse_h, lower_h, upper_h, coupling_h, blank_h,
    receiver_r, block_s, offset_r, weight_r, target_r,
    final_h, update_h,
    state, forcing, inverse, lower, upper, coupling, blank,
    near, update, gathered, placed, outgoing, received, pick, stacked,
    edge_out, edge_in, face,
    load_sem, out_sem, own_sem, fsend, frecv, esend, erecv, wsend, wrecv,
):
    s, c = lax.axis_index("stream"), lax.axis_index("cross")
    devices = ns * nc
    me = s * nc + c
    senders = block_s.shape[0]
    slots = devices * CAP
    span = tiles // CHUNKS

    loads = []

    def load(source, target):
        copy = pltpu.make_async_copy(source, target, load_sem.at[len(loads)])
        copy.start()
        loads.append(copy)
        return copy

    def rows_of(i):
        return pl.ds(i * tiles, tiles)

    state_loads = [load(state_h.at[:, :, i, :], state.at[:, rows_of(i), :]) for i in range(planes)]
    drive_loads = []
    for i in range(planes):
        drive_loads.append(load(forcing_h.at[:, :, i, :], forcing.at[:, rows_of(i), :]))
        drive_loads.append(load(coupling_h.at[:, i, :], coupling.at[rows_of(i), :]))
        drive_loads.append(load(blank_h.at[:, i, :], blank.at[rows_of(i), :]))
    sweep_loads = []
    for i in range(planes):
        sweep_loads.append(load(lower_h.at[:, :, i, :], lower.at[:, rows_of(i), :]))
        for a in range(NV):
            first = pair(a, a)
            sweep_loads.append(
                load(
                    inverse_h.at[a, pl.ds(a, NV - a), :, i, :],
                    inverse.at[pl.ds(first, NV - a), rows_of(i), :],
                )
            )
    for i in range(planes):
        sweep_loads.append(load(upper_h.at[:, :, i, :], upper.at[:, rows_of(i), :]))

    barrier = pltpu.get_barrier_semaphore()

    def greet(k, carry):
        other = lax.rem(me + k, devices)
        pl.semaphore_signal(
            barrier, inc=1, device_id=(other // nc, lax.rem(other, nc)), device_id_type=MESH
        )
        return carry

    lax.fori_loop(1, devices, greet, 0)

    eye = iota((senders, senders), 0) == iota((senders, senders), 1)
    recv_col = receiver_r[...].astype(jnp.float32)
    recv_row = jnp.sum(jnp.where(eye, recv_col, 0.0), axis=0, keepdims=True)
    earlier = iota((senders, senders), 0) < iota((senders, senders), 1)
    rank_row = jnp.sum(
        jnp.where(earlier & (recv_col == recv_row), 1.0, 0.0), axis=0, keepdims=True
    )
    key_row = rank_row * devices + recv_row
    place = (key_row == iota((slots, senders), 0).astype(jnp.float32)).astype(jnp.float32)
    place3 = jnp.concatenate([place, place, place], axis=1).astype(jnp.bfloat16)
    offset_col = jnp.sum(
        jnp.where(eye, offset_r[...].astype(jnp.float32), 0.0), axis=1, keepdims=True
    ).astype(jnp.int32)
    offset_all = jnp.broadcast_to(offset_col, (senders, 128))

    slot_eye = iota((slots, slots), 0) == iota((slots, slots), 1)
    target_col = jnp.sum(
        jnp.where(slot_eye, target_r[...].astype(jnp.float32), 0.0), axis=1, keepdims=True
    )
    slot_k = iota((slots, slots), 1)
    wanted = jnp.where(slot_k < devices, slot_k * CAP, (slot_k - devices) * CAP + 1)
    target_row = jnp.sum(
        jnp.where(iota((slots, slots), 0) == wanted, target_col, 0.0), axis=0, keepdims=True
    )
    target3 = jnp.concatenate([target_row, target_row, target_row], axis=1)

    def fill(i, carry):
        ids = (iota((tiles, 3 * slots), 0) + i * tiles).astype(jnp.float32)
        pick[pl.ds(pl.multiple_of(i * tiles, tiles), tiles), :] = jnp.where(
            ids == target3, 1.0, 0.0
        ).astype(jnp.bfloat16)
        return carry

    lax.fori_loop(0, planes, fill, 0)
    for it in range(ITERS):
        for r in range(NV * CAP, SLOT_ROWS):
            outgoing[it, pl.ds(r, devices, stride=SLOT_ROWS), :] = jnp.zeros(
                (devices, 128), jnp.float32
            )

    for copy in state_loads:
        copy.wait()
    pl.semaphore_wait(barrier, devices - 1)

    def fringe_copy(it, k):
        other = lax.rem(me + k, devices)
        start = pl.multiple_of(other * SLOT_ROWS, SLOT_ROWS)
        mine = pl.multiple_of(me * SLOT_ROWS, SLOT_ROWS)
        return pltpu.make_async_remote_copy(
            src_ref=outgoing.at[it, pl.ds(start, SLOT_ROWS), :],
            dst_ref=received.at[it, pl.ds(mine, SLOT_ROWS), :],
            send_sem=fsend.at[it, k],
            recv_sem=frecv.at[it, k],
            device_id=(other // nc, lax.rem(other, nc)),
            device_id_type=MESH,
        )

    def edge_copy(it, side):
        other = lax.rem(c + 1, nc) if side == 0 else lax.rem(c + nc - 1, nc)
        return pltpu.make_async_remote_copy(
            src_ref=edge_out.at[it, side],
            dst_ref=edge_in.at[it, side],
            send_sem=esend.at[it, side],
            recv_sem=erecv.at[it, side],
            device_id=(s, other),
            device_id_type=MESH,
        )

    def wave_copy(it, down, part):
        rows = pl.ds(part * span, span)
        if down:
            source = near.at[:, pl.ds((planes - 1) * tiles + part * span, span), :]
            other = lax.rem(s + 1, ns)
        else:
            source = update.at[:, rows, :]
            other = lax.rem(s + ns - 1, ns)
        way = 0 if down else 1
        return pltpu.make_async_remote_copy(
            src_ref=source,
            dst_ref=face.at[it, way, :, rows, :],
            send_sem=wsend.at[it, way, part],
            recv_sem=wrecv.at[it, way, part],
            device_id=(other, c),
            device_id_type=MESH,
        )

    def start_face(it, way, part):
        at_end = (s == 0) if way == 0 else (s == ns - 1)

        @pl.when(at_end)
        def _():
            face[it, way, :, pl.ds(part * span, span), :] = jnp.zeros(
                (NV, span, 128), jnp.float32
            )

        @pl.when(jnp.logical_not(at_end))
        def _():
            wave_copy(it, way == 0, part).wait_recv()

    def apply(rows, vector):
        out = []
        for a in range(NV):
            total = None
            for b in range(NV):
                term = inverse[pair(a, b), rows, :] * vector[b]
                total = term if total is None else total + term
            out.append(total)
        return out

    def sweep_down(it, part):
        start_face(it, 0, part)

        def step(g, carry):
            base = part * span + g * STEP
            x = [face[it, 0, v, pl.ds(base, STEP), :] for v in range(NV)]
            for i in range(planes):
                rows = pl.ds(i * tiles + base, STEP)
                t = [near[v, rows, :] + lower[v, rows, :] * x[v] for v in range(NV)]
                x = apply(rows, t)
                for v in range(NV):
                    near[v, rows, :] = x[v]
            return carry

        for g in range(span // STEP):
            step(g, 0)

        @pl.when(s < ns - 1)
        def _():
            wave_copy(it, True, part).start()

    def out_copies(part):
        copies = []
        for i in range(planes):
            rows = pl.ds(i * tiles + part * span, span)
            for n, (source, target) in enumerate(((state, final_h), (update, update_h))):
                copies.append(
                    pltpu.make_async_copy(
                        source.at[:, rows, :],
                        target.at[:, pl.ds(part * span, span), i, :],
                        out_sem.at[part, i, n],
                    )
                )
        return copies

    def sweep_up(it, part):
        start_face(it, 1, part)

        def step(g, carry):
            base = part * span + g * STEP
            y = [face[it, 1, v, pl.ds(base, STEP), :] for v in range(NV)]
            for i in reversed(range(planes)):
                rows = pl.ds(i * tiles + base, STEP)
                t = [upper[v, rows, :] * y[v] for v in range(NV)]
                z = apply(rows, t)
                y = [near[v, rows, :] + z[v] for v in range(NV)]
                for v in range(NV):
                    update[v, rows, :] = y[v]
                    state[v, rows, :] = state[v, rows, :] + y[v]
            return carry

        for g in range(span // STEP):
            step(g, 0)

        @pl.when(s > 0)
        def _():
            wave_copy(it, False, part).start()

        if it == ITERS - 1:
            for copy in out_copies(part):
                copy.start()

    for it in range(ITERS):
        for v in range(NV):
            edge_out[it, 0, v] = state[v, pl.ds(tiles - 1, planes, stride=tiles), :]
            edge_out[it, 1, v] = state[v, pl.ds(0, planes, stride=tiles), :]
        for side in range(2):
            edge_copy(it, side).start()

        def gather(q, carry):
            for k in range(8):
                e = q * 8 + k
                block = block_s[e]
                for v in range(NV):
                    gathered[v, pl.ds(e, 1), :] = state[v, pl.ds(block, 1), :]
            return carry

        lax.fori_loop(0, senders // 8, gather, 0)
        weight = weight_r[...]
        for v in range(NV):
            chosen = gathered[v]
            moved = chosen
            for bit in range(7):
                rolled = pltpu.roll(moved, 128 - (1 << bit), 1)
                moved = jnp.where((offset_all & (1 << bit)) != 0, rolled, moved)
            placed[:, v * 128:(v + 1) * 128] = split3(weight * (chosen + moved))
        slot_values = jnp.dot(place3, placed[...], preferred_element_type=jnp.float32)
        for v in range(NV):
            for k in range(CAP):
                outgoing[it, pl.ds(v * CAP + k, devices, stride=SLOT_ROWS), :] = slot_values[
                    k * devices:(k + 1) * devices, v * 128:(v + 1) * 128
                ]

        def send(k, carry):
            fringe_copy(it, k).start()
            return carry

        lax.fori_loop(1, devices, send, 0)
        mine = pl.ds(pl.multiple_of(me * SLOT_ROWS, SLOT_ROWS), SLOT_ROWS)
        received[it, mine, :] = outgoing[it, mine, :]

        if it == 0:
            for copy in drive_loads:
                copy.wait()
        else:
            for part in range(CHUNKS):
                @pl.when(s < ns - 1)
                def _():
                    wave_copy(it - 1, True, part).wait_send()

                @pl.when(s > 0)
                def _():
                    wave_copy(it - 1, False, part).wait_send()
        for side in range(2):
            edge_copy(it, side).wait_recv()
        lane = iota((tiles, 128), 1)
        row = iota((tiles, 128), 0)

        def drive(i, carry):
            rows = pl.ds(pl.multiple_of(i * tiles, tiles), tiles)
            factor = coupling[rows, :]
            for v in range(NV):
                x = state[v, rows, :]
                before = pltpu.roll(edge_in[it, 0, v, pl.ds(i, 1), :], 1, 1)
                after = pltpu.roll(edge_in[it, 1, v, pl.ds(i, 1), :], 127, 1)
                left = pltpu.roll(x, 1, 1)
                left = jnp.where(
                    lane == 0, jnp.where(row == 0, before, pltpu.roll(left, 1, 0)), left
                )
                right = pltpu.roll(x, 127, 1)
                right = jnp.where(
                    lane == 127,
                    jnp.where(row == tiles - 1, after, pltpu.roll(right, tiles - 1, 0)),
                    right,
                )
                near[v, rows, :] = forcing[v, rows, :] - factor * (2.0 * x - left - right)
            return carry

        lax.fori_loop(0, planes, drive, 0)

        def take(k, carry):
            fringe_copy(it, k).wait_recv()
            return carry

        lax.fori_loop(1, devices, take, 0)
        for v in range(NV):
            parts = [
                received[it, pl.ds(v * CAP + k, devices, stride=SLOT_ROWS), :] for k in range(CAP)
            ]
            stacked[:, v * 128:(v + 1) * 128] = split3(jnp.concatenate(parts, axis=0))

        def add_fringe(i, carry):
            rows = pl.ds(pl.multiple_of(i * tiles, tiles), tiles)
            hole = (1 - blank[rows, :]).astype(jnp.float32)
            fringe = jnp.dot(pick[rows, :], stacked[...], preferred_element_type=jnp.float32)
            for v in range(NV):
                near[v, rows, :] = near[v, rows, :] + hole * fringe[:, v * 128:(v + 1) * 128]
            return carry

        lax.fori_loop(0, planes, add_fringe, 0)

        if it == 0:
            for copy in sweep_loads:
                copy.wait()
        for part in range(CHUNKS):
            sweep_down(it, part)

            @pl.when(s == ns - 1)
            def _():
                sweep_up(it, part)

        @pl.when(s < ns - 1)
        def _():
            for part in range(CHUNKS):
                sweep_up(it, part)

        for side in range(2):
            edge_copy(it, side).wait_send()

        def sent(k, carry):
            fringe_copy(it, k).wait_send()
            return carry

        lax.fori_loop(1, devices, sent, 0)

    for part in range(CHUNKS):
        @pl.when(s < ns - 1)
        def _():
            wave_copy(ITERS - 1, True, part).wait_send()

        @pl.when(s > 0)
        def _():
            wave_copy(ITERS - 1, False, part).wait_send()

        for copy in out_copies(part):
            copy.wait()


def shards(
    initial_state, forcing, block_inverse, lower_decay, upper_decay, cross_coupling, iblank,
    donor_receiver, donor_block, stencil_offset, stencil_weight, fringe_target,
):
    ns, nc = lax.axis_size("stream"), lax.axis_size("cross")
    devices = ns * nc
    planes, cells = initial_state.shape[1:]
    tiles = cells // 128
    senders = donor_block.shape[0]
    slots = devices * CAP

    def tiled(x):
        lead = x.shape[:-2]
        n = len(lead)
        order = tuple(range(n)) + (n + 1, n, n + 2)
        return x.reshape(lead + (planes, tiles, 128)).transpose(order)

    def untiled(x):
        return x.transpose(0, 2, 1, 3).reshape(NV, planes, cells)

    full = (NV, planes * tiles, 128)
    f32, bf16 = jnp.float32, jnp.bfloat16
    dma = pltpu.SemaphoreType.DMA
    out = jax.ShapeDtypeStruct((NV, tiles, planes, 128), f32)
    hbm = pl.BlockSpec(memory_space=pl.ANY)
    vmem = pl.BlockSpec(memory_space=pltpu.VMEM)
    smem = pl.BlockSpec(memory_space=pltpu.SMEM)
    final, update = pl.pallas_call(
        functools.partial(kernel, ns, nc, planes, tiles),
        out_shape=(out, out),
        in_specs=[hbm] * 7 + [vmem, smem, vmem, vmem, vmem],
        out_specs=(hbm, hbm),
        scratch_shapes=[
            pltpu.VMEM(full, f32),
            pltpu.VMEM(full, f32),
            pltpu.VMEM((len(PAIRS),) + full[1:], f32),
            pltpu.VMEM(full, f32),
            pltpu.VMEM(full, f32),
            pltpu.VMEM(full[1:], f32),
            pltpu.VMEM(full[1:], jnp.int32),
            pltpu.VMEM(full, f32),
            pltpu.VMEM(full, f32),
            pltpu.VMEM((NV, senders, 128), f32),
            pltpu.VMEM((3 * senders, NV * 128), bf16),
            pltpu.VMEM((ITERS, devices * SLOT_ROWS, 128), f32),
            pltpu.VMEM((ITERS, devices * SLOT_ROWS, 128), f32),
            pltpu.VMEM((planes * tiles, 3 * slots), bf16),
            pltpu.VMEM((3 * slots, NV * 128), bf16),
            pltpu.VMEM((ITERS, 2, NV, planes, 128), f32),
            pltpu.VMEM((ITERS, 2, NV, planes, 128), f32),
            pltpu.VMEM((ITERS, 2, NV, tiles, 128), f32),
            dma((planes * (4 + 2 + NV),)),
            dma((CHUNKS, planes, 2)),
            dma((1,)),
            dma((ITERS, devices)),
            dma((ITERS, devices)),
            dma((ITERS, 2)),
            dma((ITERS, 2)),
            dma((ITERS, 2, CHUNKS)),
            dma((ITERS, 2, CHUNKS)),
        ],
        compiler_params=pltpu.CompilerParams(
            collective_id=0, has_side_effects=True, vmem_limit_bytes=56 * 1024 * 1024
        ),
    )(
        tiled(initial_state), tiled(forcing), tiled(block_inverse), tiled(lower_decay),
        tiled(upper_decay), tiled(cross_coupling), tiled(iblank),
        donor_receiver, donor_block, stencil_offset.reshape(1, senders), stencil_weight,
        fringe_target.reshape(1, slots),
    )
    return untiled(final), untiled(update)


def solution(mesh):
    return jax.shard_map(
        shards,
        mesh=mesh,
        in_specs=(
            P(None, "stream", "cross"),
            P(None, "stream", "cross"),
            P(None, None, "stream", "cross"),
            P(None, "stream", "cross"),
            P(None, "stream", "cross"),
            P("stream", "cross"),
            P("stream", "cross"),
            P(("stream", "cross"), None),
            P(("stream", "cross")),
            P(("stream", "cross")),
            P(("stream", "cross"), None),
            P(("stream", "cross")),
        ),
        out_specs=(P(None, "stream", "cross"), P(None, "stream", "cross")),
        check_vma=False,
    )
```

```python
import functools

import jax
import jax.numpy as jnp
from jax import lax
from jax.experimental import pallas as pl
from jax.experimental.pallas import tpu as pltpu
from jax.sharding import PartitionSpec as P

ITERS = 2
CAP = 2
NV = 5
SLOT_ROWS = 16
STEP = 16
CHUNKS = 4
MESH = pl.DeviceIdType.MESH
PAIRS = [(a, b) for a in range(NV) for b in range(a, NV)]


def pair(a, b):
    return PAIRS.index((min(a, b), max(a, b)))


def split3(x):
    high = x.astype(jnp.bfloat16)
    rest = x - high.astype(jnp.float32)
    mid = rest.astype(jnp.bfloat16)
    low = (rest - mid.astype(jnp.float32)).astype(jnp.bfloat16)
    return jnp.concatenate([high, mid, low], axis=0)


def iota(shape, dim):
    return lax.broadcasted_iota(jnp.int32, shape, dim)


def kernel(
    ns, nc, planes, tiles,
    state_h, forcing_h, inverse_h, lower_h, upper_h, coupling_h, blank_h,
    receiver_r, block_s, offset_r, weight_r, target_r,
    final_h, update_h,
    state, forcing, inverse, lower, upper, coupling, blank,
    near, update, gathered, placed, outgoing, received, pick, stacked,
    edge_out, edge_in, face,
    load_sem, out_sem, own_sem, fsend, frecv, esend, erecv, wsend, wrecv,
):
    s, c = lax.axis_index("stream"), lax.axis_index("cross")
    devices = ns * nc
    me = s * nc + c
    senders = block_s.shape[0]
    slots = devices * CAP
    span = tiles // CHUNKS

    loads = []

    def load(source, target):
        copy = pltpu.make_async_copy(source, target, load_sem.at[len(loads)])
        copy.start()
        loads.append(copy)
        return copy

    def rows_of(i):
        return pl.ds(i * tiles, tiles)

    state_loads = [load(state_h.at[:, :, i, :], state.at[:, rows_of(i), :]) for i in range(planes)]
    drive_loads = []
    for i in range(planes):
        drive_loads.append(load(forcing_h.at[:, :, i, :], forcing.at[:, rows_of(i), :]))
        drive_loads.append(load(coupling_h.at[:, i, :], coupling.at[rows_of(i), :]))
        drive_loads.append(load(blank_h.at[:, i, :], blank.at[rows_of(i), :]))
    sweep_loads = []
    for i in range(planes):
        sweep_loads.append(load(lower_h.at[:, :, i, :], lower.at[:, rows_of(i), :]))
        for a in range(NV):
            first = pair(a, a)
            sweep_loads.append(
                load(
                    inverse_h.at[a, pl.ds(a, NV - a), :, i, :],
                    inverse.at[pl.ds(first, NV - a), rows_of(i), :],
                )
            )
    for i in range(planes):
        sweep_loads.append(load(upper_h.at[:, :, i, :], upper.at[:, rows_of(i), :]))

    barrier = pltpu.get_barrier_semaphore()

    def greet(k, carry):
        other = lax.rem(me + k, devices)
        pl.semaphore_signal(
            barrier, inc=1, device_id=(other // nc, lax.rem(other, nc)), device_id_type=MESH
        )
        return carry

    lax.fori_loop(1, devices, greet, 0)

    eye = iota((senders, senders), 0) == iota((senders, senders), 1)
    recv_row = receiver_r[...].astype(jnp.float32)
    recv_col = jnp.sum(jnp.where(eye, recv_row, 0.0), axis=1, keepdims=True)
    earlier = iota((senders, senders), 0) < iota((senders, senders), 1)
    rank_row = jnp.sum(
        jnp.where(earlier & (recv_col == recv_row), 1.0, 0.0), axis=0, keepdims=True
    )
    key_row = rank_row * devices + recv_row
    place = (key_row == iota((slots, senders), 0).astype(jnp.float32)).astype(jnp.float32)
    place3 = jnp.concatenate([place, place, place], axis=1).astype(jnp.bfloat16)
    offset_col = jnp.sum(
        jnp.where(eye, offset_r[...].astype(jnp.float32), 0.0), axis=1, keepdims=True
    ).astype(jnp.int32)
    offset_all = jnp.broadcast_to(offset_col, (senders, 128))

    slot_eye = iota((slots, slots), 0) == iota((slots, slots), 1)
    target_col = jnp.sum(
        jnp.where(slot_eye, target_r[...].astype(jnp.float32), 0.0), axis=1, keepdims=True
    )
    slot_k = iota((slots, slots), 1)
    wanted = jnp.where(slot_k < devices, slot_k * CAP, (slot_k - devices) * CAP + 1)
    target_row = jnp.sum(
        jnp.where(iota((slots, slots), 0) == wanted, target_col, 0.0), axis=0, keepdims=True
    )
    target3 = jnp.concatenate([target_row, target_row, target_row], axis=1)

    def fill(i, carry):
        ids = (iota((tiles, 3 * slots), 0) + i * tiles).astype(jnp.float32)
        pick[pl.ds(pl.multiple_of(i * tiles, tiles), tiles), :] = jnp.where(
            ids == target3, 1.0, 0.0
        ).astype(jnp.bfloat16)
        return carry

    lax.fori_loop(0, planes, fill, 0)
    for it in range(ITERS):
        for r in range(NV * CAP, SLOT_ROWS):
            outgoing[it, pl.ds(r, devices, stride=SLOT_ROWS), :] = jnp.zeros(
                (devices, 128), jnp.float32
            )

    for copy in state_loads:
        copy.wait()
    pl.semaphore_wait(barrier, devices - 1)

    def fringe_copy(it, k):
        other = lax.rem(me + k, devices)
        start = pl.multiple_of(other * SLOT_ROWS, SLOT_ROWS)
        mine = pl.multiple_of(me * SLOT_ROWS, SLOT_ROWS)
        return pltpu.make_async_remote_copy(
            src_ref=outgoing.at[it, pl.ds(start, SLOT_ROWS), :],
            dst_ref=received.at[it, pl.ds(mine, SLOT_ROWS), :],
            send_sem=fsend.at[it, k],
            recv_sem=frecv.at[it, k],
            device_id=(other // nc, lax.rem(other, nc)),
            device_id_type=MESH,
        )

    def edge_copy(it, side):
        other = lax.rem(c + 1, nc) if side == 0 else lax.rem(c + nc - 1, nc)
        return pltpu.make_async_remote_copy(
            src_ref=edge_out.at[it, side],
            dst_ref=edge_in.at[it, side],
            send_sem=esend.at[it, side],
            recv_sem=erecv.at[it, side],
            device_id=(s, other),
            device_id_type=MESH,
        )

    def wave_copy(it, down, part):
        rows = pl.ds(part * span, span)
        if down:
            source = near.at[:, pl.ds((planes - 1) * tiles + part * span, span), :]
            other = lax.rem(s + 1, ns)
        else:
            source = update.at[:, rows, :]
            other = lax.rem(s + ns - 1, ns)
        way = 0 if down else 1
        return pltpu.make_async_remote_copy(
            src_ref=source,
            dst_ref=face.at[it, way, :, rows, :],
            send_sem=wsend.at[it, way, part],
            recv_sem=wrecv.at[it, way, part],
            device_id=(other, c),
            device_id_type=MESH,
        )

    def start_face(it, way, part):
        at_end = (s == 0) if way == 0 else (s == ns - 1)

        @pl.when(at_end)
        def _():
            face[it, way, :, pl.ds(part * span, span), :] = jnp.zeros(
                (NV, span, 128), jnp.float32
            )

        @pl.when(jnp.logical_not(at_end))
        def _():
            wave_copy(it, way == 0, part).wait_recv()

    def apply(rows, vector):
        out = []
        for a in range(NV):
            total = None
            for b in range(NV):
                term = inverse[pair(a, b), rows, :] * vector[b]
                total = term if total is None else total + term
            out.append(total)
        return out

    def sweep_down(it, part):
        start_face(it, 0, part)

        def step(g, carry):
            base = part * span + g * STEP
            x = [face[it, 0, v, pl.ds(base, STEP), :] for v in range(NV)]
            for i in range(planes):
                rows = pl.ds(i * tiles + base, STEP)
                t = [near[v, rows, :] + lower[v, rows, :] * x[v] for v in range(NV)]
                x = apply(rows, t)
                for v in range(NV):
                    near[v, rows, :] = x[v]
            return carry

        for g in range(span // STEP):
            step(g, 0)

        @pl.when(s < ns - 1)
        def _():
            wave_copy(it, True, part).start()

    def out_copies(part):
        copies = []
        for i in range(planes):
            rows = pl.ds(i * tiles + part * span, span)
            for n, (source, target) in enumerate(((state, final_h), (update, update_h))):
                copies.append(
                    pltpu.make_async_copy(
                        source.at[:, rows, :],
                        target.at[:, pl.ds(part * span, span), i, :],
                        out_sem.at[part, i, n],
                    )
                )
        return copies

    def sweep_up(it, part):
        start_face(it, 1, part)

        def step(g, carry):
            base = part * span + g * STEP
            y = [face[it, 1, v, pl.ds(base, STEP), :] for v in range(NV)]
            for i in reversed(range(planes)):
                rows = pl.ds(i * tiles + base, STEP)
                t = [upper[v, rows, :] * y[v] for v in range(NV)]
                z = apply(rows, t)
                y = [near[v, rows, :] + z[v] for v in range(NV)]
                for v in range(NV):
                    update[v, rows, :] = y[v]
                    state[v, rows, :] = state[v, rows, :] + y[v]
            return carry

        for g in range(span // STEP):
            step(g, 0)

        @pl.when(s > 0)
        def _():
            wave_copy(it, False, part).start()

        if it == ITERS - 1:
            for copy in out_copies(part):
                copy.start()

    for it in range(ITERS):
        for v in range(NV):
            edge_out[it, 0, v] = state[v, pl.ds(tiles - 1, planes, stride=tiles), :]
            edge_out[it, 1, v] = state[v, pl.ds(0, planes, stride=tiles), :]
        for side in range(2):
            edge_copy(it, side).start()

        def gather(q, carry):
            for k in range(8):
                e = q * 8 + k
                block = block_s[e]
                for v in range(NV):
                    gathered[v, pl.ds(e, 1), :] = state[v, pl.ds(block, 1), :]
            return carry

        lax.fori_loop(0, senders // 8, gather, 0)
        weight = weight_r[...]
        for v in range(NV):
            chosen = gathered[v]
            moved = chosen
            for bit in range(7):
                rolled = pltpu.roll(moved, 128 - (1 << bit), 1)
                moved = jnp.where((offset_all & (1 << bit)) != 0, rolled, moved)
            placed[:, v * 128:(v + 1) * 128] = split3(weight * (chosen + moved))
        slot_values = jnp.dot(place3, placed[...], preferred_element_type=jnp.float32)
        for v in range(NV):
            for k in range(CAP):
                outgoing[it, pl.ds(v * CAP + k, devices, stride=SLOT_ROWS), :] = slot_values[
                    k * devices:(k + 1) * devices, v * 128:(v + 1) * 128
                ]

        def send(k, carry):
            fringe_copy(it, k).start()
            return carry

        lax.fori_loop(1, devices, send, 0)
        mine = pl.ds(pl.multiple_of(me * SLOT_ROWS, SLOT_ROWS), SLOT_ROWS)
        received[it, mine, :] = outgoing[it, mine, :]

        if it == 0:
            for copy in drive_loads:
                copy.wait()
        else:
            for part in range(CHUNKS):
                @pl.when(s < ns - 1)
                def _():
                    wave_copy(it - 1, True, part).wait_send()

                @pl.when(s > 0)
                def _():
                    wave_copy(it - 1, False, part).wait_send()
        for side in range(2):
            edge_copy(it, side).wait_recv()
        lane = iota((tiles, 128), 1)
        row = iota((tiles, 128), 0)

        def drive(i, carry):
            rows = pl.ds(pl.multiple_of(i * tiles, tiles), tiles)
            factor = coupling[rows, :]
            for v in range(NV):
                x = state[v, rows, :]
                before = pltpu.roll(edge_in[it, 0, v, pl.ds(i, 1), :], 1, 1)
                after = pltpu.roll(edge_in[it, 1, v, pl.ds(i, 1), :], 127, 1)
                left = pltpu.roll(x, 1, 1)
                left = jnp.where(
                    lane == 0, jnp.where(row == 0, before, pltpu.roll(left, 1, 0)), left
                )
                right = pltpu.roll(x, 127, 1)
                right = jnp.where(
                    lane == 127,
                    jnp.where(row == tiles - 1, after, pltpu.roll(right, tiles - 1, 0)),
                    right,
                )
                near[v, rows, :] = forcing[v, rows, :] - factor * (2.0 * x - left - right)
            return carry

        lax.fori_loop(0, planes, drive, 0)

        def take(k, carry):
            fringe_copy(it, k).wait_recv()
            return carry

        lax.fori_loop(1, devices, take, 0)
        for v in range(NV):
            parts = [
                received[it, pl.ds(v * CAP + k, devices, stride=SLOT_ROWS), :] for k in range(CAP)
            ]
            stacked[:, v * 128:(v + 1) * 128] = split3(jnp.concatenate(parts, axis=0))

        def add_fringe(i, carry):
            rows = pl.ds(pl.multiple_of(i * tiles, tiles), tiles)
            hole = (1 - blank[rows, :]).astype(jnp.float32)
            fringe = jnp.dot(pick[rows, :], stacked[...], preferred_element_type=jnp.float32)
            for v in range(NV):
                near[v, rows, :] = near[v, rows, :] + hole * fringe[:, v * 128:(v + 1) * 128]
            return carry

        lax.fori_loop(0, planes, add_fringe, 0)

        if it == 0:
            for copy in sweep_loads:
                copy.wait()
        for part in range(CHUNKS):
            sweep_down(it, part)

            @pl.when(s == ns - 1)
            def _():
                sweep_up(it, part)

        @pl.when(s < ns - 1)
        def _():
            for part in range(CHUNKS):
                sweep_up(it, part)

        for side in range(2):
            edge_copy(it, side).wait_send()

        def sent(k, carry):
            fringe_copy(it, k).wait_send()
            return carry

        lax.fori_loop(1, devices, sent, 0)

    for part in range(CHUNKS):
        @pl.when(s < ns - 1)
        def _():
            wave_copy(ITERS - 1, True, part).wait_send()

        @pl.when(s > 0)
        def _():
            wave_copy(ITERS - 1, False, part).wait_send()

        for copy in out_copies(part):
            copy.wait()


def shards(
    initial_state, forcing, block_inverse, lower_decay, upper_decay, cross_coupling, iblank,
    donor_receiver, donor_block, stencil_offset, stencil_weight, fringe_target,
):
    ns, nc = lax.axis_size("stream"), lax.axis_size("cross")
    devices = ns * nc
    planes, cells = initial_state.shape[1:]
    tiles = cells // 128
    senders = donor_block.shape[0]
    slots = devices * CAP

    def tiled(x):
        lead = x.shape[:-2]
        n = len(lead)
        order = tuple(range(n)) + (n + 1, n, n + 2)
        return x.reshape(lead + (planes, tiles, 128)).transpose(order)

    def untiled(x):
        return x.transpose(0, 2, 1, 3).reshape(NV, planes, cells)

    full = (NV, planes * tiles, 128)
    f32, bf16 = jnp.float32, jnp.bfloat16
    dma = pltpu.SemaphoreType.DMA
    out = jax.ShapeDtypeStruct((NV, tiles, planes, 128), f32)
    hbm = pl.BlockSpec(memory_space=pl.ANY)
    vmem = pl.BlockSpec(memory_space=pltpu.VMEM)
    smem = pl.BlockSpec(memory_space=pltpu.SMEM)
    final, update = pl.pallas_call(
        functools.partial(kernel, ns, nc, planes, tiles),
        out_shape=(out, out),
        in_specs=[hbm] * 7 + [vmem, smem, vmem, vmem, vmem],
        out_specs=(hbm, hbm),
        scratch_shapes=[
            pltpu.VMEM(full, f32),
            pltpu.VMEM(full, f32),
            pltpu.VMEM((len(PAIRS),) + full[1:], f32),
            pltpu.VMEM(full, f32),
            pltpu.VMEM(full, f32),
            pltpu.VMEM(full[1:], f32),
            pltpu.VMEM(full[1:], jnp.int32),
            pltpu.VMEM(full, f32),
            pltpu.VMEM(full, f32),
            pltpu.VMEM((NV, senders, 128), f32),
            pltpu.VMEM((3 * senders, NV * 128), bf16),
            pltpu.VMEM((ITERS, devices * SLOT_ROWS, 128), f32),
            pltpu.VMEM((ITERS, devices * SLOT_ROWS, 128), f32),
            pltpu.VMEM((planes * tiles, 3 * slots), bf16),
            pltpu.VMEM((3 * slots, NV * 128), bf16),
            pltpu.VMEM((ITERS, 2, NV, planes, 128), f32),
            pltpu.VMEM((ITERS, 2, NV, planes, 128), f32),
            pltpu.VMEM((ITERS, 2, NV, tiles, 128), f32),
            dma((planes * (4 + 2 + NV),)),
            dma((CHUNKS, planes, 2)),
            dma((1,)),
            dma((ITERS, devices)),
            dma((ITERS, devices)),
            dma((ITERS, 2)),
            dma((ITERS, 2)),
            dma((ITERS, 2, CHUNKS)),
            dma((ITERS, 2, CHUNKS)),
        ],
        compiler_params=pltpu.CompilerParams(
            collective_id=0, has_side_effects=True, vmem_limit_bytes=56 * 1024 * 1024
        ),
    )(
        tiled(initial_state), tiled(forcing), tiled(block_inverse), tiled(lower_decay),
        tiled(upper_decay), tiled(cross_coupling), tiled(iblank),
        donor_receiver.reshape(1, senders), donor_block, stencil_offset.reshape(1, senders), stencil_weight,
        fringe_target.reshape(1, slots),
    )
    return untiled(final), untiled(update)


def solution(mesh):
    return jax.shard_map(
        shards,
        mesh=mesh,
        in_specs=(
            P(None, "stream", "cross"),
            P(None, "stream", "cross"),
            P(None, None, "stream", "cross"),
            P(None, "stream", "cross"),
            P(None, "stream", "cross"),
            P("stream", "cross"),
            P("stream", "cross"),
            P(("stream", "cross"), None),
            P(("stream", "cross")),
            P(("stream", "cross")),
            P(("stream", "cross"), None),
            P(("stream", "cross")),
        ),
        out_specs=(P(None, "stream", "cross"), P(None, "stream", "cross")),
        check_vma=False,
    )
```
